128 devices in a mesh: src: 8 (over y, core), rcv: 16 (over x, z).
Axes of the slice: x: 4, y: 4, z: 4, core: 2. Of those that a mesh axis runs over, the one named last changes fastest.
Arguments:
- traces: bfloat16 [65536, 2048], P('rcv', 'src'), may hold values from -32 to 32
- tile_list: int32 [252, 2], replicated, may hold values from 0 to 31, as said below
- tile_owner: int32 [512], replicated, may hold values from 0 to 252, as said below
Outputs:
- stacked: bfloat16 [512, 64, 64, 512], P(('src', 'rcv'))
The draws below stay inside these ranges and needn't reach their ends.
Inputs may be any that keep to these rules, and one draw needn't show every extreme that they name: `tile_list`: every tile (s, r) with s <= r <= s + 8 and r < 32 appears in exactly one row. `tile_owner`: slots k with k // 4 = d belong to device d of src+rcv in mesh order; the value 252 marks an empty slot; every tile is held in exactly one slot, and some device holds 4 tiles.
All inputs are finite; a program needn't handle non-finite values.
Results may differ from the reference program's by a relative error of at most 0.0065.
Values may be sent and summed in bfloat16 or wider, within the bound.
A program may use at most 384 MiB of HBM per device.

```python
import math
import jax
import jax.numpy as jnp
from jax import lax

CHANNELS = 2048
SAMPLES = 2048
BINS = 256
LOW_BIN = 16
BLOCK = 64
REACH = 512
WINDOWS = 32
TILES = 252
SLOTS_DEV = 4
SLOTS = 512


def draw_traces(key, part):
    key = jax.random.fold_in(key, 11)
    keys = jax.random.split(key, 5)
    tone_bin = jax.random.randint(keys[0], (CHANNELS,), LOW_BIN, LOW_BIN + BINS)
    tone_phase = jax.random.uniform(keys[1], (CHANNELS,), jnp.float32, -math.pi, math.pi)
    amplitude = jnp.exp(jax.random.uniform(keys[2], (CHANNELS,), jnp.float32, math.log(0.02), math.log(0.2)))
    noise_scale = jnp.exp(jax.random.uniform(keys[3], (WINDOWS, 1, CHANNELS), jnp.float32, math.log(0.5), math.log(5.0)))
    sample_index = jnp.arange(SAMPLES, dtype=jnp.int32)
    turns = sample_index[:, None] * tone_bin[None, :] % SAMPLES
    tone = amplitude[None, :] * jnp.cos(2.0 * math.pi / SAMPLES * turns.astype(jnp.float32) + tone_phase[None, :])
    noise = jnp.clip(jax.random.normal(keys[4], (WINDOWS, SAMPLES, CHANNELS), jnp.float32), -6.0, 6.0)
    signal = tone[None, :, :] + noise * noise_scale
    return signal.reshape(WINDOWS * SAMPLES, CHANNELS).astype(jnp.bfloat16)


def draw_tile_list(key, part):
    key = jax.random.fold_in(key, 37)
    span = REACH // BLOCK
    blocks_all = CHANNELS // BLOCK
    total = (span + 1) * blocks_all
    grid = jnp.arange(total, dtype=jnp.int32)
    offset_blocks = grid // blocks_all
    first_block = grid % blocks_all
    usable = first_block + offset_blocks < blocks_all
    ranking = jax.random.permutation(key, total).astype(jnp.int32)
    scoring = jnp.where(usable, ranking, ranking + total)
    chosen = jnp.argsort(scoring, stable=True)[:TILES]
    source_block = first_block[chosen]
    target_block = source_block + offset_blocks[chosen]
    return jnp.stack([source_block, target_block], axis=1).astype(jnp.int32)


def draw_tile_owner(key, part):
    key = jax.random.fold_in(key, 23)
    key_heavy, key_rank = jax.random.split(key)
    device_count = SLOTS // SLOTS_DEV
    slot_index = jnp.arange(SLOTS, dtype=jnp.int32)
    device_of = slot_index // SLOTS_DEV
    heavy = jax.random.randint(key_heavy, (), 0, device_count)
    ranking = jax.random.permutation(key_rank, SLOTS).astype(jnp.int32)
    scoring = jnp.where(device_of == heavy, -1 - slot_index % SLOTS_DEV, ranking)
    chosen = jnp.argsort(scoring, stable=True)[:TILES]
    empty_slots = jnp.full((SLOTS,), TILES, dtype=jnp.int32)
    return empty_slots.at[chosen].set(jnp.arange(TILES, dtype=jnp.int32))


def setup_inputs(seed: int = 0) -> dict:
    key_list = jax.random.split(jax.random.key(seed), 4)
    traces = draw_traces(jax.random.fold_in(key_list[3], 71), 0)
    tile_list = draw_tile_list(jax.random.fold_in(key_list[3], 71), 0)
    tile_owner = draw_tile_owner(jax.random.fold_in(key_list[3], 71), 0)
    return {"traces": traces, "tile_list": tile_list, "tile_owner": tile_owner}


def spectral_basis():
    sample_index = jnp.arange(SAMPLES, dtype=jnp.int32)
    bin_index = LOW_BIN + jnp.arange(BINS, dtype=jnp.int32)
    turns = sample_index[:, None] * bin_index[None, :] % SAMPLES
    angle = 2.0 * math.pi / SAMPLES * turns.astype(jnp.float32)
    return jnp.concatenate([jnp.cos(angle), -jnp.sin(angle)], axis=1).astype(jnp.bfloat16)

def whiten(spectrum):
    mean_power = lax.optimization_barrier(jnp.mean(spectrum * spectrum, axis=-1, keepdims=True))
    return (spectrum * lax.rsqrt(mean_power + 1e-06)).astype(jnp.bfloat16)

def product(left, right):
    return jnp.einsum('wif,wjf->ijf', left.astype(jnp.float32), right.astype(jnp.float32))

def cross_block(source, target):
    source_re, source_im = (source[..., :BINS], source[..., BINS:])
    target_re, target_im = (target[..., :BINS], target[..., BINS:])
    real_part = (product(source_re, target_re) + product(source_im, target_im)) / WINDOWS
    imag_part = (product(source_im, target_re) - product(source_re, target_im)) / WINDOWS
    return jnp.concatenate([real_part, imag_part], axis=-1).astype(jnp.bfloat16)

def reference(traces, tile_list, tile_owner):
    basis = spectral_basis().astype(jnp.float32)
    frames = traces.reshape(WINDOWS, SAMPLES, CHANNELS)

    def one_window(frame):
        return whiten(jnp.dot(frame.astype(jnp.float32).T, basis))
    spectra = lax.map(one_window, frames)

    def one_slot(slot_value):
        index = jnp.minimum(slot_value, TILES - 1).astype(jnp.int32)
        block_pair = tile_list[index]
        source = lax.dynamic_slice_in_dim(spectra, (block_pair[0] * BLOCK).astype(jnp.int32), BLOCK, 1)
        target = lax.dynamic_slice_in_dim(spectra, (block_pair[1] * BLOCK).astype(jnp.int32), BLOCK, 1)
        filled = (slot_value < TILES).astype(jnp.bfloat16)
        return cross_block(source, target) * filled
    return lax.map(one_slot, tile_owner)
```

```python
import functools
import math

import jax
import jax.numpy as jnp
import numpy as np
from jax import lax
from jax.experimental import pallas as pl
from jax.experimental.pallas import tpu as pltpu
from jax.sharding import PartitionSpec as P

SAMPLES = 2048
BINS = 256
LOW_BIN = 16
BLOCK = 64
TILES = 252
GROUPS = BINS // 8
CHUNKS = 4
FG = GROUPS // 4 // CHUNKS
ENTRIES = 16
MESH = pl.DeviceIdType.MESH
BF16 = jnp.bfloat16
F32 = jnp.float32


def twiddles():
    k = LOW_BIN + np.arange(BINS)[:, None]
    coarse = 2.0 * math.pi * ((k * 128 * np.arange(SAMPLES // 128)[None, :]) % SAMPLES) / SAMPLES
    fine = 2.0 * math.pi * ((k * np.arange(128)[None, :]) % SAMPLES) / SAMPLES
    pad = ((0, 0), (0, 128 - SAMPLES // 128))
    tables = [np.pad(np.cos(coarse), pad), np.pad(np.sin(coarse), pad), np.cos(fine), np.sin(fine)]
    return np.stack(tables).astype(np.float32)


def transform_kernel(traces_ref, table_ref, out_ref, basis_ref):
    cos_fine, sin_fine = table_ref[2], table_ref[3]
    for step in range(SAMPLES // 128):
        cos_coarse = table_ref[0, :, step : step + 1]
        sin_coarse = table_ref[1, :, step : step + 1]
        lanes = pl.ds(step * 128, 128)
        basis_ref[:BINS, lanes] = (cos_coarse * cos_fine - sin_coarse * sin_fine).astype(BF16)
        basis_ref[BINS:, lanes] = (-(sin_coarse * cos_fine + cos_coarse * sin_fine)).astype(BF16)
    whitened = []
    for window in range(2):
        spectrum = jnp.dot(
            basis_ref[...], traces_ref[window * SAMPLES : (window + 1) * SAMPLES, :],
            preferred_element_type=F32,
        )
        power = jnp.sum(spectrum * spectrum, axis=0, keepdims=True) * (1.0 / (2 * BINS))
        whitened.append(spectrum * lax.rsqrt(power + 1e-06))
    for block in range(4):
        lanes = slice(block * BLOCK, (block + 1) * BLOCK)
        rows = [
            jnp.concatenate([w[:BINS, lanes], w[BINS:, lanes]], axis=1).reshape(GROUPS, 8, 128)
            for w in whitened
        ]
        out_ref[block] = jnp.concatenate(rows, axis=1).astype(BF16)


def transform(traces):
    return pl.pallas_call(
        transform_kernel,
        name="transform",
        out_shape=jax.ShapeDtypeStruct((4, GROUPS, 16, 128), BF16),
        in_specs=[pl.BlockSpec(memory_space=pltpu.VMEM)] * 2,
        out_specs=pl.BlockSpec(memory_space=pltpu.VMEM),
        scratch_shapes=[pltpu.VMEM((2 * BINS, SAMPLES), BF16)],
        compiler_params=pltpu.CompilerParams(vmem_limit_bytes=40 * 2**20),
    )(traces, twiddles())


def gather_kernel(owner_ref, tiles_ref, spec_ref, out_ref, *scratch):
    count = 2 * CHUNKS
    held = scratch[:count]
    stage = scratch[count : 2 * count]
    final = scratch[2 * count : 3 * count]
    swap_s, swap_r, one_s, one_r, two_s, two_r, three_s, three_r, sib_s, sib_r, out_s = scratch[3 * count :]
    src, rcv = lax.axis_index("src"), lax.axis_index("rcv")
    y, core, x, z = src // 2, src % 2, rcv // 4, rcv % 4

    def device(axis, step):
        if axis == "core":
            return (y * 2 + (1 - core), rcv)
        if axis == "x":
            return (src, (x + step) % 4 * 4 + z)
        if axis == "y":
            return ((y + step) % 4 * 2 + core, rcv)
        return (src, x * 4 + (z + step) % 4)

    partners = [device("core", 0)] + [device(a, s) for a in "xyz" for s in (1, 2, 3)]
    barrier = pltpu.get_barrier_semaphore()
    for partner in partners:
        pl.semaphore_signal(barrier, inc=1, device_id=partner, device_id_type=MESH)

    for c in range(CHUNKS):
        for q in range(2):
            n = 2 * c + q
            mine = (x, z)[q]
            start = core * (GROUPS // 2) + q * (GROUPS // 4) + c * FG
            for block in range(4):
                held[n][y, mine, core * 4 + block] = spec_ref[block, pl.ds(start, FG)]
    pl.semaphore_wait(barrier, len(partners))

    sent = []

    def send(source, target, send_sem, recv_sem, to):
        copy = pltpu.make_async_remote_copy(
            src_ref=source, dst_ref=target, send_sem=send_sem, recv_sem=recv_sem,
            device_id=to, device_id_type=MESH,
        )
        copy.start()
        sent.append(copy)
        return copy

    order = [(c, q) for c in range(CHUNKS) for q in range(2)]
    swaps, ones, twos, threes, sibs, outs = {}, {}, {}, {}, {}, {}
    for c, q in order:
        n = 2 * c + q
        mine = (x, z)[q]
        start = (1 - core) * (GROUPS // 2) + q * (GROUPS // 4) + c * FG
        swaps[n] = send(
            spec_ref.at[:, pl.ds(start, FG)], held[n].at[y, mine, pl.ds(core * 4, 4)],
            swap_s.at[n], swap_r.at[n], device("core", 0),
        )
    for c, q in order:
        n = 2 * c + q
        mine = (x, z)[q]
        swaps[n].wait_recv()
        part = held[n].at[y, mine]
        ones[n] = [
            send(part, part, one_s.at[n, s - 1], one_r.at[n, s - 1], device("xz"[q], s))
            for s in (1, 3, 2)
        ]
    for c, q in order:
        n = 2 * c + q
        for copy in ones[n]:
            copy.wait_recv()
        part = held[n].at[y]
        twos[n] = [
            send(part, part, two_s.at[n, s - 1], two_r.at[n, s - 1], device("y", s))
            for s in (1, 3, 2)
        ]

    def finish(n):
        c, q = n // 2, n % 2
        for copy in threes[n]:
            copy.wait_recv()
        local = pltpu.make_async_copy(
            final[n].at[:, pl.ds(core * 8, 8)], out_ref.at[core, q, c], out_s.at[n]
        )
        local.start()
        outs[n] = local
        sibs[n] = send(
            final[n].at[:, pl.ds((1 - core) * 8, 8)], out_ref.at[core, q, c],
            sib_s.at[n], sib_r.at[n], device("core", 0),
        )

    for position, (c, q) in enumerate(order):
        n = 2 * c + q
        for copy in twos[n]:
            copy.wait_recv()
        last = (z, x)[q]

        def pick(e, step):
            there = (last + step) % 4
            to_rcv = (x * 4 + there, there * 4 + z)[q]
            slot = ((y * 2 + e // 8) * 16 + to_rcv) * 4 + e % 8 // 2
            tile = jnp.minimum(owner_ref[slot], TILES - 1)
            block = tiles_ref[2 * tile + e % 2]
            return held[n][block // 8, :, block % 8]

        for step in range(4):

            @pl.loop(0, ENTRIES)
            def _(e, step=step):
                if step:
                    stage[n][step - 1, e] = pick(e, step)
                else:
                    final[n][last, e] = pick(e, step)

        threes[n] = [
            send(
                stage[n].at[s - 1], final[n].at[last],
                three_s.at[n, s - 1], three_r.at[n, s - 1], device("zx"[q], s),
            )
            for s in (1, 3, 2)
        ]
        if position:
            finish(2 * order[position - 1][0] + order[position - 1][1])
    finish(2 * order[-1][0] + order[-1][1])
    for n in range(count):
        sibs[n].wait_recv()
        outs[n].wait()
    for copy in sent:
        copy.wait_send()


def gather(owner, tiles, spec):
    count = 2 * CHUNKS
    tail = (FG, 16, 128)
    dma = pltpu.SemaphoreType.DMA
    return pl.pallas_call(
        gather_kernel,
        name="gather",
        out_shape=jax.ShapeDtypeStruct((2, 2, CHUNKS, 4, 8, 4) + tail, BF16),
        in_specs=[
            pl.BlockSpec(memory_space=pltpu.SMEM),
            pl.BlockSpec(memory_space=pltpu.SMEM),
            pl.BlockSpec(memory_space=pltpu.VMEM),
        ],
        out_specs=pl.BlockSpec(memory_space=pl.ANY),
        scratch_shapes=[pltpu.VMEM((4, 4, 8) + tail, BF16)] * count
        + [pltpu.VMEM((3, ENTRIES, 4) + tail, BF16)] * count
        + [pltpu.VMEM((4, ENTRIES, 4) + tail, BF16)] * count
        + [dma((count,))] * 2
        + [dma((count, 3))] * 6
        + [dma((count,))] * 3,
        compiler_params=pltpu.CompilerParams(
            collective_id=0, has_side_effects=True, vmem_limit_bytes=56 * 2**20
        ),
    )(owner, tiles, spec)


def correlate_kernel(owner_ref, source_ref, target_ref, out_ref, cross_ref):
    slot, half = pl.program_id(0), pl.program_id(1)
    filled = owner_ref[slot] < TILES
    lane = lax.broadcasted_iota(jnp.int32, (BLOCK, 512), 1) % 8
    positive = lax.broadcasted_iota(jnp.int32, (256, 128), 1) < BLOCK
    sign = jnp.where(positive, 1.0, -1.0).astype(BF16)

    @pl.when(filled)
    def _():
        @pl.loop(0, 2 * CHUNKS, unroll=8 // FG)
        def _(step):
            q, c = step // CHUNKS, step % CHUNKS
            for group in range(FG):
                source = source_ref[0, q, c, :, 0, :, group].reshape(256, 128).T
                target = target_ref[0, q, c, :, 0, :, group].reshape(256, 128)
                left = jnp.concatenate([source[:BLOCK], source[BLOCK:]], axis=1)
                left = jnp.concatenate([jnp.where(lane == f, left, BF16(0)) for f in range(8)], axis=0)
                turned = jnp.concatenate([target[:, BLOCK:], target[:, :BLOCK]], axis=1)
                right = jnp.concatenate([target * sign, turned], axis=0)
                cross = jnp.dot(left, right, preferred_element_type=F32) * (1.0 / 32)
                first = pl.multiple_of(q * 64 + (c * FG + group) * 8, 8)
                cross_ref[:, pl.ds(first, 8), :] = jnp.swapaxes(cross.reshape(8, BLOCK, 128), 0, 1)

        @pl.loop(0, BLOCK, unroll=16)
        def _(i):
            turned = cross_ref[i].astype(BF16).T
            out_ref[0, i, :, pl.ds(pl.multiple_of(half * 128, 128), 128)] = turned[:BLOCK]
            out_ref[0, i, :, pl.ds(pl.multiple_of(BINS + half * 128, 128), 128)] = turned[BLOCK:]

    @pl.when(jnp.logical_not(filled))
    def _():
        out_ref[...] = jnp.zeros_like(out_ref)


def correlate(owner, received):
    block = (1, 2, CHUNKS, 4, 1, 4, FG, 16, 128)

    def side(role):
        return pl.BlockSpec(block, lambda s, k, own: (k, 0, 0, 0, 2 * s + role, 0, 0, 0, 0))

    return pl.pallas_call(
        correlate_kernel,
        name="correlate",
        out_shape=jax.ShapeDtypeStruct((4, BLOCK, BLOCK, 2 * BINS), BF16),
        grid_spec=pltpu.PrefetchScalarGridSpec(
            num_scalar_prefetch=1,
            grid=(4, 2),
            in_specs=[side(0), side(1)],
            out_specs=pl.BlockSpec((1, BLOCK, BLOCK, 2 * BINS), lambda s, k, own: (s, 0, 0, 0)),
            scratch_shapes=[pltpu.VMEM((BLOCK, 128, 128), F32)],
        ),
        compiler_params=pltpu.CompilerParams(vmem_limit_bytes=40 * 2**20),
    )(owner, received, received)


def per_device(traces, tile_list, tile_owner):
    spec = transform(traces)
    received = gather(tile_owner, tile_list.reshape(-1), spec)
    first = (lax.axis_index("src") * lax.axis_size("rcv") + lax.axis_index("rcv")) * 4
    return correlate(lax.dynamic_slice_in_dim(tile_owner, first, 4), received)


def solution(mesh):
    in_specs = (P("rcv", "src"), P(), P())
    out_specs = P(("src", "rcv"), None, None, None)
    return jax.shard_map(
        per_device, mesh=mesh, in_specs=in_specs, out_specs=out_specs, check_vma=False
    )
```

```python
import functools
import math

import jax
import jax.numpy as jnp
import numpy as np
from jax import lax
from jax.experimental import pallas as pl
from jax.experimental.pallas import tpu as pltpu
from jax.sharding import PartitionSpec as P

SAMPLES = 2048
BINS = 256
LOW_BIN = 16
BLOCK = 64
TILES = 252
GROUPS = BINS // 8
CHUNKS = GROUPS // 4
COUNT = 2 * CHUNKS
ENTRIES = 16
NONE = 32
CAPS = (12, 14, 16)
AHEAD_ONE = 4
AHEAD_TWO = 3
AHEAD_FWD = 1
LAG = 4
STAGES = 8
MESH = pl.DeviceIdType.MESH
BF16 = jnp.bfloat16
F32 = jnp.float32


def twiddles():
    k = LOW_BIN + np.arange(BINS)[:, None]
    coarse = 2.0 * math.pi * ((k * 128 * np.arange(SAMPLES // 128)[None, :]) % SAMPLES) / SAMPLES
    fine = 2.0 * math.pi * ((k * np.arange(128)[None, :]) % SAMPLES) / SAMPLES
    both = np.concatenate([np.cos(coarse), np.sin(coarse)], axis=1)
    both = np.pad(both, ((0, 0), (0, 128 - both.shape[1])))
    return np.stack([both, np.cos(fine), np.sin(fine)]).astype(np.float32)


def fill_basis(table_ref, basis_ref):
    cos_fine, sin_fine = table_ref[1], table_ref[2]
    for step in range(SAMPLES // 128):
        cos_coarse = table_ref[0, :, step : step + 1]
        sin_coarse = table_ref[0, :, 16 + step : 17 + step]
        lanes = pl.ds(step * 128, 128)
        basis_ref[:BINS, lanes] = (cos_coarse * cos_fine - sin_coarse * sin_fine).astype(BF16)
        basis_ref[BINS:, lanes] = (-(sin_coarse * cos_fine + cos_coarse * sin_fine)).astype(BF16)


def transform(frame, basis_ref):
    spectrum = jnp.dot(basis_ref[...], frame, preferred_element_type=F32)
    power = jnp.sum(spectrum * spectrum, axis=0, keepdims=True) * (1.0 / (2 * BINS))
    return spectrum * lax.rsqrt(power + 1e-06)


def correlate(source, target):
    lane = lax.broadcasted_iota(jnp.int32, (BLOCK, 512), 1) % 8
    positive = lax.broadcasted_iota(jnp.int32, (256, 128), 1) < BLOCK
    sign = jnp.where(positive, 1.0, -1.0).astype(BF16)
    source = source.T
    left = jnp.concatenate([source[:BLOCK], source[BLOCK:]], axis=1)
    left = jnp.concatenate([jnp.where(lane == f, left, BF16(0)) for f in range(8)], axis=0)
    turned = jnp.concatenate([target[:, BLOCK:], target[:, :BLOCK]], axis=1)
    right = jnp.concatenate([target * sign, turned], axis=0)
    product = jnp.dot(left, right, preferred_element_type=F32) * (1.0 / 32)
    return jnp.swapaxes(product.reshape(8, BLOCK, 128), 0, 1)


def cross_kernel(cap, owner_ref, tiles_ref, table_ref, traces_ref, out_ref, *scratch):
    held = scratch[:COUNT]
    final = scratch[COUNT : 2 * COUNT]
    stage = scratch[2 * COUNT : 2 * COUNT + STAGES]
    cross, list_ref, place_ref, frames, basis, spec = scratch[2 * COUNT + STAGES : 2 * COUNT + STAGES + 6]
    (load_s, swap_s, swap_r, one_s, one_r, two_s, two_r, fwd_s, fwd_r,
     three_s, three_r, sib_s, sib_r, out_s) = scratch[2 * COUNT + STAGES + 6 :]
    src, rcv = lax.axis_index("src"), lax.axis_index("rcv")
    y, core, x, z = src // 2, src % 2, rcv // 4, rcv % 4

    def device(axis, step):
        if axis == "core":
            return (y * 2 + (1 - core), rcv)
        if axis == "x":
            return (src, (x + step) % 4 * 4 + z)
        if axis == "y":
            return ((y + step) % 4 * 2 + core, rcv)
        return (src, x * 4 + (z + step) % 4)

    partners = [device("core", 0)] + [device(a, s) for a in "xz" for s in (1, 2, 3)]
    partners += [device("y", 1), device("y", 3)]
    barrier = pltpu.get_barrier_semaphore()
    for partner in partners:
        pl.semaphore_signal(barrier, inc=1, device_id=partner, device_id_type=MESH)

    loads = [
        pltpu.make_async_copy(traces_ref.at[pl.ds(w * SAMPLES, SAMPLES)], frames.at[w], load_s.at[w])
        for w in range(2)
    ]
    for load in loads:
        load.start()
    fill_basis(table_ref, basis)
    whitened = []
    for w in range(2):
        loads[w].wait()
        whitened.append(transform(frames[w], basis))
    for block in range(4):
        lanes = slice(block * BLOCK, (block + 1) * BLOCK)
        rows = [
            jnp.concatenate([v[:BINS, lanes], v[BINS:, lanes]], axis=1).reshape(GROUPS, 8, 128)
            for v in whitened
        ]
        spec[block] = jnp.concatenate(rows, axis=1).astype(BF16)

    for n in range(COUNT):
        group = core * (GROUPS // 2) + n % 2 * CHUNKS + n // 2
        for block in range(4):
            held[n][y, (x, z)[n % 2], core * 4 + block] = spec[block, group]
    pl.semaphore_wait(barrier, len(partners))

    sent = []

    def send(source, target, send_sem, recv_sem, to, keep=True):
        copy = pltpu.make_async_remote_copy(
            src_ref=source, dst_ref=target, send_sem=send_sem, recv_sem=recv_sem,
            device_id=to, device_id_type=MESH,
        )
        copy.start()
        if keep:
            sent.append(copy)
        return copy

    swaps, ones, twos, forwards, threes, sibs, outs = {}, {}, {}, {}, {}, {}, {}

    def start_one(n):
        swaps[n].wait_recv()
        part = held[n].at[y, (x, z)[n % 2]]
        ones[n] = [
            send(part, part, one_s.at[n, s - 1], one_r.at[n, s - 1], device("xz"[n % 2], s))
            for s in (1, 3, 2)
        ]

    def start_two(n):
        for copy in ones[n]:
            copy.wait_recv()
        part = held[n].at[y]
        twos[n] = [
            send(part, part, two_s.at[n, i], two_r.at[n, i], device("y", s))
            for i, s in enumerate((1, 3))
        ]

    def start_forward(n):
        forwards[n] = []
        for i, s in enumerate((1, 3)):
            twos[n][i].wait_recv()
            part = held[n].at[(y - s) % 4, pl.ds(2 * i, 2)]
            forwards[n].append(send(part, part, fwd_s.at[n, i], fwd_r.at[n, i], device("y", s)))

    def start_three(n):
        q = n % 2
        for copy in forwards[n]:
            copy.wait_recv()
        last = (z, x)[q]
        parcel = stage[n % STAGES]
        if n >= STAGES:
            for copy in threes[n - STAGES]:
                copy.wait_send()

        def pick(row, r):
            block = list_ref[row, r]
            return held[n][block // 8, :, block % 8]

        @pl.loop(0, cap)
        def _(r):
            final[n][last, r] = pick(0, r)
            for s in (1, 2, 3):
                parcel[s - 1, r] = pick(s + 3 * q, r)

        threes[n] = [
            send(
                parcel.at[s - 1], final[n].at[last],
                three_s.at[n, s - 1], three_r.at[n, s - 1], device("zx"[q], s),
                keep=n >= COUNT - STAGES,
            )
            for s in (1, 3, 2)
        ]

    def finish(unit, mine):
        q, m = unit % 2, unit // 2
        pair = (4 * m + q, 4 * m + 2 + q)
        if not mine:
            for n in pair:
                for copy in threes[n]:
                    copy.wait_recv()
        if unit >= 2:
            if mine:
                outs[unit - 2].wait()
            else:
                sibs[unit - 2].wait_send()
        first = (core if mine else 1 - core) * 4
        there = out_ref.at[core * CHUNKS + q * (CHUNKS // 2) + m]
        buffer = cross.at[unit % 2, int(mine)]

        @pl.loop(0, 4, unroll=2)
        def _(j):
            parts = []
            for n in pair:
                source = final[n][:, place_ref[2 * (first + j)]].reshape(256, 128)
                target = final[n][:, place_ref[2 * (first + j) + 1]].reshape(256, 128)
                parts.append(correlate(source, target))
            buffer[j] = jnp.concatenate(parts, axis=1).astype(BF16)

        if mine:
            outs[unit] = pltpu.make_async_copy(buffer, there, out_s.at[unit])
            outs[unit].start()
        else:
            sibs[unit] = send(
                buffer, there, sib_s.at[unit], sib_r.at[unit], device("core", 0),
                keep=unit >= CHUNKS - 2,
            )

    for n in range(COUNT):
        group = (1 - core) * (GROUPS // 2) + n % 2 * CHUNKS + n // 2
        swaps[n] = send(
            spec.at[:, group], held[n].at[y, (x, z)[n % 2], pl.ds(core * 4, 4)],
            swap_s.at[n], swap_r.at[n], device("core", 0),
        )
    for n in range(AHEAD_ONE):
        start_one(n)
    for n in range(AHEAD_TWO):
        start_two(n)
        start_one(AHEAD_ONE + n)

    @pl.loop(0, 7)
    def _(turn_index):
        row = 6 - turn_index
        to_x = (x + jnp.where(row > 3, row - 3, 0)) % 4
        to_z = (z + jnp.where(row > 3, 0, row)) % 4
        blocks = []
        for slot in range(ENTRIES // 2):
            tile = owner_ref[((y * 2 + slot // 4) * 16 + to_x * 4 + to_z) * 4 + slot % 4]
            for role in range(2):
                block = tiles_ref[role, jnp.minimum(tile, TILES - 1)]
                blocks.append(jnp.where(tile < TILES, block, NONE))
        places = [jnp.int32(0)] * ENTRIES
        previous = jnp.int32(-1)
        for r in range(cap):
            current = jnp.int32(NONE)
            for block in blocks:
                current = jnp.minimum(current, jnp.where(block > previous, block, NONE))
            places = [p + jnp.where(current < b, 1, 0) for p, b in zip(places, blocks)]
            list_ref[row, r] = jnp.where(current < NONE, current, 0)
            previous = current
        for e in range(ENTRIES):
            place_ref[e] = jnp.minimum(places[e], cap - 1)

    for n in range(AHEAD_FWD):
        start_forward(n)
    work = [(u, mine) for u in range(CHUNKS) for mine in (False, True)]
    for n in range(COUNT):
        if n + AHEAD_ONE + AHEAD_TWO < COUNT:
            start_one(n + AHEAD_ONE + AHEAD_TWO)
        if n + AHEAD_TWO < COUNT:
            start_two(n + AHEAD_TWO)
        if n + AHEAD_FWD < COUNT:
            start_forward(n + AHEAD_FWD)
        start_three(n)
        u = work[0][0]
        if 4 * (u // 2) + 2 + u % 2 <= n - LAG:
            finish(*work.pop(0))
    while work:
        finish(*work.pop(0))
    for unit in range(CHUNKS):
        sibs[unit].wait_recv()
    for unit in (CHUNKS - 2, CHUNKS - 1):
        outs[unit].wait()
    for copy in sent:
        copy.wait_send()


def cross_spectra(cap, owner, tiles, traces):
    tail = (16, 128)
    dma = pltpu.SemaphoreType.DMA
    return pl.pallas_call(
        functools.partial(cross_kernel, cap),
        name=f"cross_{cap}",
        out_shape=jax.ShapeDtypeStruct((2 * CHUNKS, 4, BLOCK, 16, 128), BF16),
        in_specs=[
            pl.BlockSpec(memory_space=pltpu.SMEM),
            pl.BlockSpec(memory_space=pltpu.SMEM),
            pl.BlockSpec(memory_space=pltpu.VMEM),
            pl.BlockSpec(memory_space=pl.ANY),
        ],
        out_specs=pl.BlockSpec(memory_space=pl.ANY),
        scratch_shapes=[pltpu.VMEM((4, 4, 8) + tail, BF16)] * COUNT
        + [pltpu.VMEM((4, cap, 4) + tail, BF16)] * COUNT
        + [pltpu.VMEM((3, cap, 4) + tail, BF16)] * STAGES
        + [pltpu.VMEM((2, 2, 4, BLOCK, 16, 128), BF16)]
        + [pltpu.SMEM((7, cap), jnp.int32), pltpu.SMEM((ENTRIES,), jnp.int32)]
        + [pltpu.VMEM((2, SAMPLES, 4 * BLOCK), BF16)]
        + [pltpu.VMEM((2 * BINS, SAMPLES), BF16)]
        + [pltpu.VMEM((4, GROUPS) + tail, BF16)]
        + [dma((2,))]
        + [dma((COUNT,))] * 2
        + [dma((COUNT, 3))] * 2
        + [dma((COUNT, 2))] * 4
        + [dma((COUNT, 3))] * 2
        + [dma((CHUNKS,))] * 3,
        compiler_params=pltpu.CompilerParams(
            collective_id=cap, has_side_effects=True, vmem_limit_bytes=(28 + cap) * 2**20
        ),
    )(owner, tiles, twiddles(), traces)


def turn_kernel(rows, owner_ref, cross_ref, out_ref):
    first = (lax.axis_index("src") * 16 + lax.axis_index("rcv")) * 4
    filled = owner_ref[first + pl.program_id(0)] < TILES

    @pl.when(filled)
    def _():
        @pl.loop(0, rows, unroll=16)
        def _(i):
            turned = cross_ref[:, 0, i].reshape(BINS, 128).T
            out_ref[0, i, :, :BINS] = turned[:BLOCK]
            out_ref[0, i, :, BINS:] = turned[BLOCK:]

    @pl.when(jnp.logical_not(filled))
    def _():
        out_ref[...] = jnp.zeros_like(out_ref)


def turn(owner, cross):
    rows = BLOCK
    return pl.pallas_call(
        functools.partial(turn_kernel, rows),
        name="turn",
        out_shape=jax.ShapeDtypeStruct((4, BLOCK, BLOCK, 2 * BINS), BF16),
        grid_spec=pltpu.PrefetchScalarGridSpec(
            num_scalar_prefetch=1,
            grid=(4, BLOCK // rows),
            in_specs=[pl.BlockSpec((2 * CHUNKS, 1, rows, 16, 128), lambda s, i, own: (0, s, i, 0, 0))],
            out_specs=pl.BlockSpec((1, rows, BLOCK, 2 * BINS), lambda s, i, own: (s, i, 0, 0)),
        ),
        compiler_params=pltpu.CompilerParams(vmem_limit_bytes=60 * 2**20),
    )(owner, cross)


def most_blocks(owner, tiles):
    ones = jnp.left_shift(1, tiles[:, 0]) | jnp.left_shift(1, tiles[:, 1])
    picked = owner[:, None] == jnp.arange(TILES, dtype=jnp.int32)[None, :]
    named = jnp.sum(jnp.where(picked, ones[None, :], 0), axis=1).reshape(4, 2, 16, 4)
    named = lax.reduce(named, np.int32(0), lax.bitwise_or, (1, 3))
    return jnp.max(lax.population_count(named))


def per_device(traces, tile_list, tile_owner):
    def run(cap):
        return lambda traces, tiles, owner: turn(owner, cross_spectra(cap, owner, tiles, traces))

    most = most_blocks(tile_owner, tile_list)
    index = sum((most > cap).astype(jnp.int32) for cap in CAPS[:-1])
    return lax.switch(index, [run(cap) for cap in CAPS], traces, tile_list.T, tile_owner)


def solution(mesh):
    in_specs = (P("rcv", "src"), P(), P())
    out_specs = P(("src", "rcv"), None, None, None)
    return jax.shard_map(
        per_device, mesh=mesh, in_specs=in_specs, out_specs=out_specs, check_vma=False
    )
```

```python
import functools
import math

import jax
import jax.numpy as jnp
import numpy as np
from jax import lax
from jax.experimental import pallas as pl
from jax.experimental.pallas import tpu as pltpu
from jax.sharding import PartitionSpec as P

SAMPLES = 2048
BINS = 256
LOW_BIN = 16
BLOCK = 64
TILES = 252
GROUPS = BINS // 8
CHUNKS = GROUPS // 4
COUNT = 2 * CHUNKS
ENTRIES = 16
NONE = 32
CAPS = (11, 12, 13, 14, 16)
AHEAD_TWO = 2
AHEAD_FWD = 1
LAG = 4
STAGES = 8
MESH = pl.DeviceIdType.MESH
BF16 = jnp.bfloat16
F32 = jnp.float32


def twiddles():
    k = LOW_BIN + np.arange(BINS)[:, None]
    coarse = 2.0 * math.pi * ((k * 128 * np.arange(SAMPLES // 128)[None, :]) % SAMPLES) / SAMPLES
    fine = 2.0 * math.pi * ((k * np.arange(128)[None, :]) % SAMPLES) / SAMPLES
    both = np.concatenate([np.cos(coarse), np.sin(coarse)], axis=1)
    both = np.pad(both, ((0, 0), (0, 128 - both.shape[1])))
    return np.stack([both, np.cos(fine), np.sin(fine)]).astype(np.float32)


def fill_basis(table_ref, basis_ref):
    cos_fine, sin_fine = table_ref[1], table_ref[2]
    for step in range(SAMPLES // 128):
        cos_coarse = table_ref[0, :, step : step + 1]
        sin_coarse = table_ref[0, :, 16 + step : 17 + step]
        lanes = pl.ds(step * 128, 128)
        basis_ref[:BINS, lanes] = (cos_coarse * cos_fine - sin_coarse * sin_fine).astype(BF16)
        basis_ref[BINS:, lanes] = (-(sin_coarse * cos_fine + cos_coarse * sin_fine)).astype(BF16)


def transform(frame, basis_ref):
    spectrum = jnp.dot(basis_ref[...], frame, preferred_element_type=F32)
    power = jnp.sum(spectrum * spectrum, axis=0, keepdims=True) * (1.0 / (2 * BINS))
    return spectrum * lax.rsqrt(power + 1e-06)


def correlate(source, target):
    lane = lax.broadcasted_iota(jnp.int32, (BLOCK, 512), 1) % 8
    positive = lax.broadcasted_iota(jnp.int32, (256, 128), 1) < BLOCK
    sign = jnp.where(positive, 1.0, -1.0).astype(BF16)
    source = source.T
    left = jnp.concatenate([source[:BLOCK], source[BLOCK:]], axis=1)
    left = jnp.concatenate([jnp.where(lane == f, left, BF16(0)) for f in range(8)], axis=0)
    turned = jnp.concatenate([target[:, BLOCK:], target[:, :BLOCK]], axis=1)
    right = jnp.concatenate([target * sign, turned], axis=0)
    product = jnp.dot(left, right, preferred_element_type=F32) * (1.0 / 32)
    return jnp.swapaxes(product.reshape(8, BLOCK, 128), 0, 1)


def cross_kernel(cap, owner_ref, tiles_ref, table_hbm, traces_ref, out_ref, *scratch):
    held = scratch[:COUNT]
    final = scratch[COUNT : 2 * COUNT]
    stage = scratch[2 * COUNT : 2 * COUNT + STAGES]
    cross, early, list_ref, place_ref, frames, basis, spec, table_ref = scratch[2 * COUNT + STAGES : 2 * COUNT + STAGES + 8]
    (load_s, swap_s, swap_r, one_s, one_r, two_s, two_r, fwd_s, fwd_r,
     three_s, three_r, sib_s, sib_r, out_s) = scratch[2 * COUNT + STAGES + 8 :]
    src, rcv = lax.axis_index("src"), lax.axis_index("rcv")
    y, core, x, z = src // 2, src % 2, rcv // 4, rcv % 4

    def device(axis, step):
        if axis == "core":
            return (y * 2 + (1 - core), rcv)
        if axis == "x":
            return (src, (x + step) % 4 * 4 + z)
        if axis == "y":
            return ((y + step) % 4 * 2 + core, rcv)
        return (src, x * 4 + (z + step) % 4)

    partners = [device("core", 0)] + [device(a, s) for a in "xz" for s in (1, 2, 3)]
    partners += [device("y", 1), device("y", 3)]
    barrier = pltpu.get_barrier_semaphore()
    for partner in partners:
        pl.semaphore_signal(barrier, inc=1, device_id=partner, device_id_type=MESH)

    loads = [
        pltpu.make_async_copy(traces_ref.at[pl.ds(w * SAMPLES, SAMPLES)], frames.at[w], load_s.at[w])
        for w in range(2)
    ]
    load_table = pltpu.make_async_copy(table_hbm, table_ref, load_s.at[2])
    load_table.start()
    for load in loads:
        load.start()
    load_table.wait()
    fill_basis(table_ref, basis)
    whitened = []
    for w in range(2):
        loads[w].wait()
        whitened.append(transform(frames[w], basis))
    for block in range(4):
        lanes = slice(block * BLOCK, (block + 1) * BLOCK)
        rows = [
            jnp.concatenate([v[:BINS, lanes], v[BINS:, lanes]], axis=1).reshape(GROUPS, 8, 128)
            for v in whitened
        ]
        spec[block] = jnp.concatenate(rows, axis=1).astype(BF16)

    for n in range(COUNT):
        group = core * (GROUPS // 2) + n % 2 * CHUNKS + n // 2
        for block in range(4):
            held[n][y, (x, z)[n % 2], core * 4 + block] = spec[block, group]
    pl.semaphore_wait(barrier, len(partners))

    sent = []

    def send(source, target, send_sem, recv_sem, to, keep=True):
        copy = pltpu.make_async_remote_copy(
            src_ref=source, dst_ref=target, send_sem=send_sem, recv_sem=recv_sem,
            device_id=to, device_id_type=MESH,
        )
        copy.start()
        if keep:
            sent.append(copy)
        return copy

    swaps, ones, twos, forwards, threes, sibs, outs = {}, {}, {}, {}, {}, {}, {}

    def start_one(n):
        swaps[n].wait_recv()
        part = held[n].at[y, (x, z)[n % 2]]
        ones[n] = [
            send(part, part, one_s.at[n, s - 1], one_r.at[n, s - 1], device("xz"[n % 2], s))
            for s in (1, 3, 2)
        ]

    def start_two(n):
        for copy in ones[n]:
            copy.wait_recv()
        part = held[n].at[y]
        twos[n] = [
            send(part, part, two_s.at[n, i], two_r.at[n, i], device("y", s))
            for i, s in enumerate((1, 3))
        ]

    def start_forward(n):
        forwards[n] = []
        for i, s in enumerate((1, 3)):
            twos[n][i].wait_recv()
            part = held[n].at[(y - s) % 4, pl.ds(2 * i, 2)]
            forwards[n].append(send(part, part, fwd_s.at[n, i], fwd_r.at[n, i], device("y", s)))

    def start_three(n):
        q = n % 2
        for copy in forwards[n]:
            copy.wait_recv()
        last = (z, x)[q]
        parcel = stage[n % STAGES]
        if n >= STAGES:
            for copy in threes[n - STAGES]:
                copy.wait_send()

        def pick(row, r):
            block = list_ref[row, r]
            return held[n][block // 8, :, block % 8]

        @pl.loop(0, cap)
        def _(r):
            final[n][last, r] = pick(0, r)
            for s in (1, 2, 3):
                parcel[s - 1, r] = pick(s + 3 * q, r)

        threes[n] = [
            send(
                parcel.at[s - 1], final[n].at[last],
                three_s.at[n, s - 1], three_r.at[n, s - 1], device("zx"[q], s),
                keep=n >= COUNT - STAGES,
            )
            for s in (1, 3, 2)
        ]

    def product(n, slot):
        source = final[n][:, place_ref[2 * slot]].reshape(256, 128)
        target = final[n][:, place_ref[2 * slot + 1]].reshape(256, 128)
        return correlate(source, target)

    def finish(unit, part):
        q, m = unit % 2, unit // 2
        n = 4 * m + q + (2 if part else 0)
        if part < 2:
            for copy in threes[n]:
                copy.wait_recv()
        if not part:

            @pl.loop(0, 8, unroll=2)
            def _(slot):
                early[q, slot] = product(n, slot)

            return
        mine = part == 2
        if unit >= 2:
            if mine:
                outs[unit - 2].wait()
            else:
                sibs[unit - 2].wait_send()
        first = (core if mine else 1 - core) * 4
        buffer = cross.at[unit % 2, int(mine)]

        @pl.loop(0, 4, unroll=2)
        def _(j):
            both = [early[q, first + j], product(n, first + j)]
            buffer[j] = jnp.concatenate(both, axis=1).astype(BF16)

        there = out_ref.at[core * CHUNKS + q * (CHUNKS // 2) + m]
        if mine:
            outs[unit] = pltpu.make_async_copy(buffer, there, out_s.at[unit])
            outs[unit].start()
        else:
            sibs[unit] = send(
                buffer, there, sib_s.at[unit], sib_r.at[unit], device("core", 0),
                keep=unit >= CHUNKS - 2,
            )

    for n in range(COUNT):
        group = (1 - core) * (GROUPS // 2) + n % 2 * CHUNKS + n // 2
        swaps[n] = send(
            spec.at[:, group], held[n].at[y, (x, z)[n % 2], pl.ds(core * 4, 4)],
            swap_s.at[n], swap_r.at[n], device("core", 0),
        )
    for n in range(COUNT):
        start_one(n)
    for n in range(AHEAD_TWO):
        start_two(n)

    @pl.loop(0, 7)
    def _(turn_index):
        row = 6 - turn_index
        to_x = (x + jnp.where(row > 3, row - 3, 0)) % 4
        to_z = (z + jnp.where(row > 3, 0, row)) % 4
        blocks = []
        for slot in range(ENTRIES // 2):
            tile = owner_ref[((y * 2 + slot // 4) * 16 + to_x * 4 + to_z) * 4 + slot % 4]
            for role in range(2):
                block = tiles_ref[role, jnp.minimum(tile, TILES - 1)]
                blocks.append(jnp.where(tile < TILES, block, NONE))
        places = [jnp.int32(0)] * ENTRIES
        previous = jnp.int32(-1)
        for r in range(cap):
            current = jnp.int32(NONE)
            for block in blocks:
                current = jnp.minimum(current, jnp.where(block > previous, block, NONE))
            places = [p + jnp.where(current < b, 1, 0) for p, b in zip(places, blocks)]
            list_ref[row, r] = jnp.where(current < NONE, current, 0)
            previous = current
        for e in range(ENTRIES):
            place_ref[e] = jnp.minimum(places[e], cap - 1)

    for n in range(AHEAD_FWD):
        start_forward(n)
    work = [(u + q, part) for u in range(0, CHUNKS, 2) for q, part in ((0, 0), (1, 0), (0, 1), (0, 2), (1, 1), (1, 2))]
    for n in range(COUNT):
        if n + AHEAD_TWO < COUNT:
            start_two(n + AHEAD_TWO)
        if n + AHEAD_FWD < COUNT:
            start_forward(n + AHEAD_FWD)
        start_three(n)
        done = 0
        while work and done < 2:
            unit, part = work[0]
            if 4 * (unit // 2) + unit % 2 + (2 if part else 0) > n - LAG:
                break
            finish(*work.pop(0))
            done += 1 if part else 2
    while work:
        finish(*work.pop(0))
    for unit in range(CHUNKS):
        sibs[unit].wait_recv()
    for unit in (CHUNKS - 2, CHUNKS - 1):
        outs[unit].wait()
    for copy in sent:
        copy.wait_send()


def cross_spectra(cap, owner, tiles, traces):
    tail = (16, 128)
    dma = pltpu.SemaphoreType.DMA
    return pl.pallas_call(
        functools.partial(cross_kernel, cap),
        name=f"cross_{cap}",
        out_shape=jax.ShapeDtypeStruct((2 * CHUNKS, 4, BLOCK, 16, 128), BF16),
        in_specs=[
            pl.BlockSpec(memory_space=pltpu.SMEM),
            pl.BlockSpec(memory_space=pltpu.SMEM),
            pl.BlockSpec(memory_space=pl.ANY),
            pl.BlockSpec(memory_space=pl.ANY),
        ],
        out_specs=pl.BlockSpec(memory_space=pl.ANY),
        scratch_shapes=[pltpu.VMEM((4, 4, 8) + tail, BF16)] * COUNT
        + [pltpu.VMEM((4, cap, 4) + tail, BF16)] * COUNT
        + [pltpu.VMEM((3, cap, 4) + tail, BF16)] * STAGES
        + [pltpu.VMEM((2, 2, 4, BLOCK, 16, 128), BF16)]
        + [pltpu.VMEM((2, ENTRIES // 2, BLOCK, 8, 128), F32)]
        + [pltpu.SMEM((7, cap), jnp.int32), pltpu.SMEM((ENTRIES,), jnp.int32)]
        + [pltpu.VMEM((2, SAMPLES, 4 * BLOCK), BF16)]
        + [pltpu.VMEM((2 * BINS, SAMPLES), BF16)]
        + [pltpu.VMEM((4, GROUPS) + tail, BF16)]
        + [pltpu.VMEM((3, BINS, 128), F32)]
        + [dma((3,))]
        + [dma((COUNT,))] * 2
        + [dma((COUNT, 3))] * 2
        + [dma((COUNT, 2))] * 4
        + [dma((COUNT, 3))] * 2
        + [dma((CHUNKS,))] * 3,
        compiler_params=pltpu.CompilerParams(
            collective_id=cap, has_side_effects=True, vmem_limit_bytes=60 * 2**20
        ),
    )(owner, tiles, twiddles(), traces)


def turn_kernel(rows, owner_ref, cross_ref, out_ref):
    first = (lax.axis_index("src") * 16 + lax.axis_index("rcv")) * 4
    filled = owner_ref[first + pl.program_id(0)] < TILES

    @pl.when(filled)
    def _():
        @pl.loop(0, rows, unroll=16)
        def _(i):
            turned = cross_ref[:, 0, i].reshape(BINS, 128).T
            out_ref[0, i, :, :BINS] = turned[:BLOCK]
            out_ref[0, i, :, BINS:] = turned[BLOCK:]

    @pl.when(jnp.logical_not(filled))
    def _():
        out_ref[...] = jnp.zeros_like(out_ref)


def turn(owner, cross):
    rows = BLOCK
    return pl.pallas_call(
        functools.partial(turn_kernel, rows),
        name="turn",
        out_shape=jax.ShapeDtypeStruct((4, BLOCK, BLOCK, 2 * BINS), BF16),
        grid_spec=pltpu.PrefetchScalarGridSpec(
            num_scalar_prefetch=1,
            grid=(4, BLOCK // rows),
            in_specs=[pl.BlockSpec((2 * CHUNKS, 1, rows, 16, 128), lambda s, i, own: (0, s, i, 0, 0))],
            out_specs=pl.BlockSpec((1, rows, BLOCK, 2 * BINS), lambda s, i, own: (s, i, 0, 0)),
        ),
        compiler_params=pltpu.CompilerParams(vmem_limit_bytes=60 * 2**20),
    )(owner, cross)


def most_blocks(owner, tiles):
    ones = jnp.left_shift(1, tiles[:, 0]) | jnp.left_shift(1, tiles[:, 1])
    picked = owner[:, None] == jnp.arange(TILES, dtype=jnp.int32)[None, :]
    named = jnp.sum(jnp.where(picked, ones[None, :], 0), axis=1).reshape(4, 2, 16, 4)
    named = lax.reduce(named, np.int32(0), lax.bitwise_or, (1, 3))
    return jnp.max(lax.population_count(named))


def per_device(traces, tile_list, tile_owner):
    def run(cap):
        return lambda traces, tiles, owner: turn(owner, cross_spectra(cap, owner, tiles, traces))

    most = most_blocks(tile_owner, tile_list)
    index = sum((most > cap).astype(jnp.int32) for cap in CAPS[:-1])
    return lax.switch(index, [run(cap) for cap in CAPS], traces, tile_list.T, tile_owner)


def solution(mesh):
    in_specs = (P("rcv", "src"), P(), P())
    out_specs = P(("src", "rcv"), None, None, None)
    return jax.shard_map(
        per_device, mesh=mesh, in_specs=in_specs, out_specs=out_specs, check_vma=False
    )
```

```python
import functools
import math

import jax
import jax.numpy as jnp
import numpy as np
from jax import lax
from jax.experimental import pallas as pl
from jax.experimental.pallas import tpu as pltpu
from jax.sharding import PartitionSpec as P

SAMPLES = 2048
BINS = 256
LOW_BIN = 16
BLOCK = 64
TILES = 252
GROUPS = BINS // 8
CHUNKS = GROUPS // 4
COUNT = 2 * CHUNKS
ENTRIES = 16
NONE = 32
CAPS = (12, 13, 14, 16)
AHEAD_TWO = 2
AHEAD_FWD = 1
LAG = 4
STAGES = 8
MESH = pl.DeviceIdType.MESH
BF16 = jnp.bfloat16
F32 = jnp.float32


def twiddles():
    k = LOW_BIN + np.arange(BINS)[:, None]
    coarse = 2.0 * math.pi * ((k * 128 * np.arange(SAMPLES // 128)[None, :]) % SAMPLES) / SAMPLES
    fine = 2.0 * math.pi * ((k * np.arange(128)[None, :]) % SAMPLES) / SAMPLES
    both = np.concatenate([np.cos(coarse), np.sin(coarse)], axis=1)
    both = np.pad(both, ((0, 0), (0, 128 - both.shape[1])))
    return np.stack([both, np.cos(fine), np.sin(fine)]).astype(np.float32)


def fill_basis(table_ref, basis_ref):
    cos_fine, sin_fine = table_ref[1], table_ref[2]
    for step in range(SAMPLES // 128):
        cos_coarse = table_ref[0, :, step : step + 1]
        sin_coarse = table_ref[0, :, 16 + step : 17 + step]
        lanes = pl.ds(step * 128, 128)
        basis_ref[:BINS, lanes] = (cos_coarse * cos_fine - sin_coarse * sin_fine).astype(BF16)
        basis_ref[BINS:, lanes] = (-(sin_coarse * cos_fine + cos_coarse * sin_fine)).astype(BF16)


def transform(frame, basis_ref):
    spectrum = jnp.dot(basis_ref[...], frame, preferred_element_type=F32)
    power = jnp.sum(spectrum * spectrum, axis=0, keepdims=True) * (1.0 / (2 * BINS))
    return spectrum * lax.rsqrt(power + 1e-06)


def correlate(source, target):
    lane = lax.broadcasted_iota(jnp.int32, (BLOCK, 512), 1) % 8
    positive = lax.broadcasted_iota(jnp.int32, (256, 128), 1) < BLOCK
    sign = jnp.where(positive, 1.0, -1.0).astype(BF16)
    source = source.T
    left = jnp.concatenate([source[:BLOCK], source[BLOCK:]], axis=1)
    left = jnp.concatenate([jnp.where(lane == f, left, BF16(0)) for f in range(8)], axis=0)
    turned = jnp.concatenate([target[:, BLOCK:], target[:, :BLOCK]], axis=1)
    right = jnp.concatenate([target * sign, turned], axis=0)
    product = jnp.dot(left, right, preferred_element_type=F32) * (1.0 / 32)
    return jnp.swapaxes(product.reshape(8, BLOCK, 128), 0, 1)


def cross_kernel(cap, owner_ref, tiles_ref, table_hbm, traces_ref, out_ref, *scratch):
    held = scratch[:COUNT]
    final = scratch[COUNT : 2 * COUNT]
    stage = scratch[2 * COUNT : 2 * COUNT + STAGES]
    cross, early, list_ref, place_ref, frames, basis, spec, table_ref = scratch[2 * COUNT + STAGES : 2 * COUNT + STAGES + 8]
    (load_s, swap_s, swap_r, one_s, one_r, two_s, two_r, fwd_s, fwd_r,
     three_s, three_r, sib_s, sib_r, out_s) = scratch[2 * COUNT + STAGES + 8 :]
    src, rcv = lax.axis_index("src"), lax.axis_index("rcv")
    y, core, x, z = src // 2, src % 2, rcv // 4, rcv % 4

    def device(axis, step):
        if axis == "core":
            return (y * 2 + (1 - core), rcv)
        if axis == "x":
            return (src, (x + step) % 4 * 4 + z)
        if axis == "y":
            return ((y + step) % 4 * 2 + core, rcv)
        return (src, x * 4 + (z + step) % 4)

    partners = [device("core", 0)] + [device(a, s) for a in "xz" for s in (1, 2, 3)]
    partners += [device("y", 1), device("y", 3)]
    barrier = pltpu.get_barrier_semaphore()
    for partner in partners:
        pl.semaphore_signal(barrier, inc=1, device_id=partner, device_id_type=MESH)

    loads = [
        pltpu.make_async_copy(traces_ref.at[pl.ds(w * SAMPLES, SAMPLES)], frames.at[w], load_s.at[w])
        for w in range(2)
    ]
    load_table = pltpu.make_async_copy(table_hbm, table_ref, load_s.at[2])
    load_table.start()
    for load in loads:
        load.start()
    load_table.wait()
    fill_basis(table_ref, basis)
    whitened = []
    for w in range(2):
        loads[w].wait()
        whitened.append(transform(frames[w], basis))
    for block in range(4):
        lanes = slice(block * BLOCK, (block + 1) * BLOCK)
        rows = [
            jnp.concatenate([v[:BINS, lanes], v[BINS:, lanes]], axis=1).reshape(GROUPS, 8, 128)
            for v in whitened
        ]
        spec[block] = jnp.concatenate(rows, axis=1).astype(BF16)

    for n in range(COUNT):
        group = core * (GROUPS // 2) + n % 2 * CHUNKS + n // 2
        for block in range(4):
            held[n][y, (x, z)[n % 2], core * 4 + block] = spec[block, group]
    pl.semaphore_wait(barrier, len(partners))

    sent = []

    def send(source, target, send_sem, recv_sem, to, keep=True):
        copy = pltpu.make_async_remote_copy(
            src_ref=source, dst_ref=target, send_sem=send_sem, recv_sem=recv_sem,
            device_id=to, device_id_type=MESH,
        )
        copy.start()
        if keep:
            sent.append(copy)
        return copy

    swaps, ones, twos, forwards, threes, sibs, outs = {}, {}, {}, {}, {}, {}, {}

    def start_one(n):
        swaps[n].wait_recv()
        part = held[n].at[y, (x, z)[n % 2]]
        ones[n] = [
            send(part, part, one_s.at[n, s - 1], one_r.at[n, s - 1], device("xz"[n % 2], s))
            for s in (1, 3, 2)
        ]

    def start_two(n):
        for copy in ones[n]:
            copy.wait_recv()
        part = held[n].at[y]
        twos[n] = [
            send(part, part, two_s.at[n, i], two_r.at[n, i], device("y", s))
            for i, s in enumerate((1, 3))
        ]

    def start_forward(n):
        forwards[n] = []
        for i, s in enumerate((1, 3)):
            twos[n][i].wait_recv()
            part = held[n].at[(y - s) % 4, pl.ds(2 * i, 2)]
            forwards[n].append(send(part, part, fwd_s.at[n, i], fwd_r.at[n, i], device("y", s)))

    def start_three(n):
        q = n % 2
        for copy in forwards[n]:
            copy.wait_recv()
        last = (z, x)[q]
        parcel = stage[n % STAGES]
        if n >= STAGES:
            for copy in threes[n - STAGES]:
                copy.wait_send()

        def pick(row, r):
            block = list_ref[row, r]
            return held[n][block // 8, :, block % 8]

        @pl.loop(0, cap)
        def _(r):
            final[n][last, r] = pick(0, r)
            for s in (1, 2, 3):
                parcel[s - 1, r] = pick(s + 3 * q, r)

        threes[n] = [
            send(
                parcel.at[s - 1], final[n].at[last],
                three_s.at[n, s - 1], three_r.at[n, s - 1], device("zx"[q], s),
                keep=n >= COUNT - STAGES,
            )
            for s in (1, 3, 2)
        ]

    def product(n, slot):
        source = final[n][:, place_ref[2 * slot]].reshape(256, 128)
        target = final[n][:, place_ref[2 * slot + 1]].reshape(256, 128)
        return correlate(source, target)

    def finish(unit, part):
        q, m = unit % 2, unit // 2
        n = 4 * m + q + (2 if part else 0)
        if part < 2:
            for copy in threes[n]:
                copy.wait_recv()
        if not part:

            @pl.loop(0, 8, unroll=2)
            def _(slot):
                early[q, slot] = product(n, slot)

            return
        mine = part == 2
        if unit >= 2:
            if mine:
                outs[unit - 2].wait()
            else:
                sibs[unit - 2].wait_send()
        first = (core if mine else 1 - core) * 4
        buffer = cross.at[unit % 2, int(mine)]

        @pl.loop(0, 4, unroll=2)
        def _(j):
            both = [early[q, first + j], product(n, first + j)]
            buffer[j] = jnp.concatenate(both, axis=1).astype(BF16)

        there = out_ref.at[core * CHUNKS + q * (CHUNKS // 2) + m]
        if mine:
            outs[unit] = pltpu.make_async_copy(buffer, there, out_s.at[unit])
            outs[unit].start()
        else:
            sibs[unit] = send(
                buffer, there, sib_s.at[unit], sib_r.at[unit], device("core", 0),
                keep=unit >= CHUNKS - 2,
            )

    for n in range(COUNT):
        group = (1 - core) * (GROUPS // 2) + n % 2 * CHUNKS + n // 2
        swaps[n] = send(
            spec.at[:, group], held[n].at[y, (x, z)[n % 2], pl.ds(core * 4, 4)],
            swap_s.at[n], swap_r.at[n], device("core", 0),
        )
    for n in range(COUNT):
        start_one(n)
    for n in range(AHEAD_TWO):
        start_two(n)

    @pl.loop(0, 7)
    def _(turn_index):
        row = 6 - turn_index
        to_x = (x + jnp.where(row > 3, row - 3, 0)) % 4
        to_z = (z + jnp.where(row > 3, 0, row)) % 4
        blocks = []
        for slot in range(ENTRIES // 2):
            tile = owner_ref[((y * 2 + slot // 4) * 16 + to_x * 4 + to_z) * 4 + slot % 4]
            for role in range(2):
                block = tiles_ref[role, jnp.minimum(tile, TILES - 1)]
                blocks.append(jnp.where(tile < TILES, block, NONE))
        places = [jnp.int32(0)] * ENTRIES
        previous = jnp.int32(-1)
        for r in range(cap):
            current = jnp.int32(NONE)
            for block in blocks:
                current = jnp.minimum(current, jnp.where(block > previous, block, NONE))
            places = [p + jnp.where(current < b, 1, 0) for p, b in zip(places, blocks)]
            list_ref[row, r] = jnp.where(current < NONE, current, 0)
            previous = current
        for e in range(ENTRIES):
            place_ref[e] = jnp.minimum(places[e], cap - 1)

    for n in range(AHEAD_FWD):
        start_forward(n)
    work = [(u + q, part) for u in range(0, CHUNKS, 2) for q, part in ((0, 0), (1, 0), (0, 1), (0, 2), (1, 1), (1, 2))]
    for n in range(COUNT):
        if n + AHEAD_TWO < COUNT:
            start_two(n + AHEAD_TWO)
        if n + AHEAD_FWD < COUNT:
            start_forward(n + AHEAD_FWD)
        start_three(n)
        done = 0
        while work and done < 2:
            unit, part = work[0]
            if 4 * (unit // 2) + unit % 2 + (2 if part else 0) > n - LAG:
                break
            finish(*work.pop(0))
            done += 1 if part else 2
    while work:
        finish(*work.pop(0))
    for unit in range(CHUNKS):
        sibs[unit].wait_recv()
    for unit in (CHUNKS - 2, CHUNKS - 1):
        outs[unit].wait()
    for copy in sent:
        copy.wait_send()


def cross_spectra(cap, owner, tiles, traces):
    tail = (16, 128)
    dma = pltpu.SemaphoreType.DMA
    return pl.pallas_call(
        functools.partial(cross_kernel, cap),
        name=f"cross_{cap}",
        out_shape=jax.ShapeDtypeStruct((2 * CHUNKS, 4, BLOCK, 16, 128), BF16),
        in_specs=[
            pl.BlockSpec(memory_space=pltpu.SMEM),
            pl.BlockSpec(memory_space=pltpu.SMEM),
            pl.BlockSpec(memory_space=pl.ANY),
            pl.BlockSpec(memory_space=pl.ANY),
        ],
        out_specs=pl.BlockSpec(memory_space=pl.ANY),
        scratch_shapes=[pltpu.VMEM((4, 4, 8) + tail, BF16)] * COUNT
        + [pltpu.VMEM((4, cap, 4) + tail, BF16)] * COUNT
        + [pltpu.VMEM((3, cap, 4) + tail, BF16)] * STAGES
        + [pltpu.VMEM((2, 2, 4, BLOCK, 16, 128), BF16)]
        + [pltpu.VMEM((2, ENTRIES // 2, BLOCK, 8, 128), F32)]
        + [pltpu.SMEM((7, cap), jnp.int32), pltpu.SMEM((ENTRIES,), jnp.int32)]
        + [pltpu.VMEM((2, SAMPLES, 4 * BLOCK), BF16)]
        + [pltpu.VMEM((2 * BINS, SAMPLES), BF16)]
        + [pltpu.VMEM((4, GROUPS) + tail, BF16)]
        + [pltpu.VMEM((3, BINS, 128), F32)]
        + [dma((3,))]
        + [dma((COUNT,))] * 2
        + [dma((COUNT, 3))] * 2
        + [dma((COUNT, 2))] * 4
        + [dma((COUNT, 3))] * 2
        + [dma((CHUNKS,))] * 3,
        compiler_params=pltpu.CompilerParams(
            collective_id=cap, has_side_effects=True, vmem_limit_bytes=60 * 2**20
        ),
    )(owner, tiles, twiddles(), traces)


def turn_kernel(rows, owner_ref, cross_ref, out_ref):
    first = (lax.axis_index("src") * 16 + lax.axis_index("rcv")) * 4
    filled = owner_ref[first + pl.program_id(0)] < TILES

    @pl.when(filled)
    def _():
        @pl.loop(0, rows, unroll=16)
        def _(i):
            turned = cross_ref[:, 0, i].reshape(BINS, 128).T
            out_ref[0, i, :, :BINS] = turned[:BLOCK]
            out_ref[0, i, :, BINS:] = turned[BLOCK:]

    @pl.when(jnp.logical_not(filled))
    def _():
        out_ref[...] = jnp.zeros_like(out_ref)


def turn(owner, cross):
    rows = BLOCK
    return pl.pallas_call(
        functools.partial(turn_kernel, rows),
        name="turn",
        out_shape=jax.ShapeDtypeStruct((4, BLOCK, BLOCK, 2 * BINS), BF16),
        grid_spec=pltpu.PrefetchScalarGridSpec(
            num_scalar_prefetch=1,
            grid=(4, BLOCK // rows),
            in_specs=[pl.BlockSpec((2 * CHUNKS, 1, rows, 16, 128), lambda s, i, own: (0, s, i, 0, 0))],
            out_specs=pl.BlockSpec((1, rows, BLOCK, 2 * BINS), lambda s, i, own: (s, i, 0, 0)),
        ),
        compiler_params=pltpu.CompilerParams(vmem_limit_bytes=60 * 2**20),
    )(owner, cross)


def most_blocks(owner, tiles):
    ones = jnp.left_shift(1, tiles[:, 0]) | jnp.left_shift(1, tiles[:, 1])
    picked = owner[:, None] == jnp.arange(TILES, dtype=jnp.int32)[None, :]
    named = jnp.sum(jnp.where(picked, ones[None, :], 0), axis=1).reshape(4, 2, 16, 4)
    named = lax.reduce(named, np.int32(0), lax.bitwise_or, (1, 3))
    return jnp.max(lax.population_count(named))


def per_device(traces, tile_list, tile_owner):
    def run(cap):
        return lambda traces, tiles, owner: turn(owner, cross_spectra(cap, owner, tiles, traces))

    most = most_blocks(tile_owner, tile_list)
    index = sum((most > cap).astype(jnp.int32) for cap in CAPS[:-1])
    return lax.switch(index, [run(cap) for cap in CAPS], traces, tile_list.T, tile_owner)


def solution(mesh):
    in_specs = (P("rcv", "src"), P(), P())
    out_specs = P(("src", "rcv"), None, None, None)
    return jax.shard_map(
        per_device, mesh=mesh, in_specs=in_specs, out_specs=out_specs, check_vma=False
    )
```

```python
import functools
import math

import jax
import jax.numpy as jnp
import numpy as np
from jax import lax
from jax.experimental import pallas as pl
from jax.experimental.pallas import tpu as pltpu
from jax.sharding import PartitionSpec as P

SAMPLES = 2048
BINS = 256
LOW_BIN = 16
BLOCK = 64
TILES = 252
GROUPS = BINS // 8
CHUNKS = GROUPS // 4
COUNT = 2 * CHUNKS
ENTRIES = 16
NONE = 32
CAPS = (13, 14, 16)
AHEAD_TWO = 2
AHEAD_FWD = 1
LAG = 4
STAGES = 8
MESH = pl.DeviceIdType.MESH
BF16 = jnp.bfloat16
F32 = jnp.float32


def twiddles():
    k = LOW_BIN + np.arange(BINS)[:, None]
    coarse = 2.0 * math.pi * ((k * 128 * np.arange(SAMPLES // 128)[None, :]) % SAMPLES) / SAMPLES
    fine = 2.0 * math.pi * ((k * np.arange(128)[None, :]) % SAMPLES) / SAMPLES
    both = np.concatenate([np.cos(coarse), np.sin(coarse)], axis=1)
    both = np.pad(both, ((0, 0), (0, 128 - both.shape[1])))
    return np.stack([both, np.cos(fine), np.sin(fine)]).astype(np.float32)


def fill_basis(table_ref, basis_ref):
    cos_fine, sin_fine = table_ref[1], table_ref[2]
    for step in range(SAMPLES // 128):
        cos_coarse = table_ref[0, :, step : step + 1]
        sin_coarse = table_ref[0, :, 16 + step : 17 + step]
        lanes = pl.ds(step * 128, 128)
        basis_ref[:BINS, lanes] = (cos_coarse * cos_fine - sin_coarse * sin_fine).astype(BF16)
        basis_ref[BINS:, lanes] = (-(sin_coarse * cos_fine + cos_coarse * sin_fine)).astype(BF16)


def transform(frame, basis_ref):
    spectrum = jnp.dot(basis_ref[...], frame, preferred_element_type=F32)
    power = jnp.sum(spectrum * spectrum, axis=0, keepdims=True) * (1.0 / (2 * BINS))
    return spectrum * lax.rsqrt(power + 1e-06)


def correlate(source, target):
    lane = lax.broadcasted_iota(jnp.int32, (BLOCK, 512), 1) % 8
    positive = lax.broadcasted_iota(jnp.int32, (256, 128), 1) < BLOCK
    sign = jnp.where(positive, 1.0, -1.0).astype(BF16)
    source = source.T
    left = jnp.concatenate([source[:BLOCK], source[BLOCK:]], axis=1)
    left = jnp.concatenate([jnp.where(lane == f, left, BF16(0)) for f in range(8)], axis=0)
    turned = jnp.concatenate([target[:, BLOCK:], target[:, :BLOCK]], axis=1)
    right = jnp.concatenate([target * sign, turned], axis=0)
    product = jnp.dot(left, right, preferred_element_type=F32) * (1.0 / 32)
    return jnp.swapaxes(product.reshape(8, BLOCK, 128), 0, 1)


def cross_kernel(cap, owner_ref, tiles_ref, table_hbm, traces_ref, out_ref, *scratch):
    held = scratch[:COUNT]
    final = scratch[COUNT : 2 * COUNT]
    stage = scratch[2 * COUNT : 2 * COUNT + STAGES]
    cross, early, list_ref, place_ref, frames, basis, spec, table_ref = scratch[2 * COUNT + STAGES : 2 * COUNT + STAGES + 8]
    (load_s, swap_s, swap_r, one_s, one_r, two_s, two_r, fwd_s, fwd_r,
     three_s, three_r, sib_s, sib_r, out_s) = scratch[2 * COUNT + STAGES + 8 :]
    src, rcv = lax.axis_index("src"), lax.axis_index("rcv")
    y, core, x, z = src // 2, src % 2, rcv // 4, rcv % 4

    def device(axis, step):
        if axis == "core":
            return (y * 2 + (1 - core), rcv)
        if axis == "x":
            return (src, (x + step) % 4 * 4 + z)
        if axis == "y":
            return ((y + step) % 4 * 2 + core, rcv)
        return (src, x * 4 + (z + step) % 4)

    partners = [device("core", 0)] + [device(a, s) for a in "xz" for s in (1, 2, 3)]
    partners += [device("y", 1), device("y", 3)]
    barrier = pltpu.get_barrier_semaphore()
    for partner in partners:
        pl.semaphore_signal(barrier, inc=1, device_id=partner, device_id_type=MESH)

    loads = [
        pltpu.make_async_copy(traces_ref.at[pl.ds(w * SAMPLES, SAMPLES)], frames.at[w], load_s.at[w])
        for w in range(2)
    ]
    load_table = pltpu.make_async_copy(table_hbm, table_ref, load_s.at[2])
    load_table.start()
    for load in loads:
        load.start()
    load_table.wait()
    fill_basis(table_ref, basis)
    whitened = []
    for w in range(2):
        loads[w].wait()
        whitened.append(transform(frames[w], basis))
    for block in range(4):
        lanes = slice(block * BLOCK, (block + 1) * BLOCK)
        rows = [
            jnp.concatenate([v[:BINS, lanes], v[BINS:, lanes]], axis=1).reshape(GROUPS, 8, 128)
            for v in whitened
        ]
        spec[block] = jnp.concatenate(rows, axis=1).astype(BF16)

    for n in range(COUNT):
        group = core * (GROUPS // 2) + n % 2 * CHUNKS + n // 2
        for block in range(4):
            held[n][y, (x, z)[n % 2], core * 4 + block] = spec[block, group]
    pl.semaphore_wait(barrier, len(partners))

    sent = []

    def send(source, target, send_sem, recv_sem, to, keep=True):
        copy = pltpu.make_async_remote_copy(
            src_ref=source, dst_ref=target, send_sem=send_sem, recv_sem=recv_sem,
            device_id=to, device_id_type=MESH,
        )
        copy.start()
        if keep:
            sent.append(copy)
        return copy

    swaps, ones, twos, forwards, threes, sibs, outs = {}, {}, {}, {}, {}, {}, {}

    def start_one(n):
        swaps[n].wait_recv()
        part = held[n].at[y, (x, z)[n % 2]]
        ones[n] = [
            send(part, part, one_s.at[n, s - 1], one_r.at[n, s - 1], device("xz"[n % 2], s))
            for s in (1, 3, 2)
        ]

    def start_two(n):
        for copy in ones[n]:
            copy.wait_recv()
        part = held[n].at[y]
        twos[n] = [
            send(part, part, two_s.at[n, i], two_r.at[n, i], device("y", s))
            for i, s in enumerate((1, 3))
        ]

    def start_forward(n):
        forwards[n] = []
        for i, s in enumerate((1, 3)):
            twos[n][i].wait_recv()
            part = held[n].at[(y - s) % 4, pl.ds(2 * i, 2)]
            forwards[n].append(send(part, part, fwd_s.at[n, i], fwd_r.at[n, i], device("y", s)))

    def start_three(n):
        q = n % 2
        for copy in forwards[n]:
            copy.wait_recv()
        last = (z, x)[q]
        parcel = stage[n % STAGES]
        if n >= STAGES:
            for copy in threes[n - STAGES]:
                copy.wait_send()

        def pick(row, r):
            block = list_ref[row, r]
            return held[n][block // 8, :, block % 8]

        @pl.loop(0, cap)
        def _(r):
            final[n][last, r] = pick(0, r)
            for s in (1, 2, 3):
                parcel[s - 1, r] = pick(s + 3 * q, r)

        threes[n] = [
            send(
                parcel.at[s - 1], final[n].at[last],
                three_s.at[n, s - 1], three_r.at[n, s - 1], device("zx"[q], s),
                keep=n >= COUNT - STAGES,
            )
            for s in (1, 3, 2)
        ]

    def product(n, slot):
        source = final[n][:, place_ref[2 * slot]].reshape(256, 128)
        target = final[n][:, place_ref[2 * slot + 1]].reshape(256, 128)
        return correlate(source, target)

    def finish(unit, part):
        q, m = unit % 2, unit // 2
        n = 4 * m + q + (2 if part else 0)
        if part < 2:
            for copy in threes[n]:
                copy.wait_recv()
        if not part:

            @pl.loop(0, 8, unroll=2)
            def _(slot):
                early[q, slot] = product(n, slot)

            return
        mine = part == 2
        if unit >= 2:
            if mine:
                outs[unit - 2].wait()
            else:
                sibs[unit - 2].wait_send()
        first = (core if mine else 1 - core) * 4
        buffer = cross.at[unit % 2, int(mine)]

        @pl.loop(0, 4, unroll=2)
        def _(j):
            both = [early[q, first + j], product(n, first + j)]
            buffer[j] = jnp.concatenate(both, axis=1).astype(BF16)

        there = out_ref.at[core * CHUNKS + q * (CHUNKS // 2) + m]
        if mine:
            outs[unit] = pltpu.make_async_copy(buffer, there, out_s.at[unit])
            outs[unit].start()
        else:
            sibs[unit] = send(
                buffer, there, sib_s.at[unit], sib_r.at[unit], device("core", 0),
                keep=unit >= CHUNKS - 2,
            )

    for n in range(COUNT):
        group = (1 - core) * (GROUPS // 2) + n % 2 * CHUNKS + n // 2
        swaps[n] = send(
            spec.at[:, group], held[n].at[y, (x, z)[n % 2], pl.ds(core * 4, 4)],
            swap_s.at[n], swap_r.at[n], device("core", 0),
        )
    for n in range(COUNT):
        start_one(n)
    for n in range(AHEAD_TWO):
        start_two(n)

    @pl.loop(0, 7)
    def _(turn_index):
        row = 6 - turn_index
        to_x = (x + jnp.where(row > 3, row - 3, 0)) % 4
        to_z = (z + jnp.where(row > 3, 0, row)) % 4
        blocks = []
        for slot in range(ENTRIES // 2):
            tile = owner_ref[((y * 2 + slot // 4) * 16 + to_x * 4 + to_z) * 4 + slot % 4]
            for role in range(2):
                block = tiles_ref[role, jnp.minimum(tile, TILES - 1)]
                blocks.append(jnp.where(tile < TILES, block, NONE))
        places = [jnp.int32(0)] * ENTRIES
        previous = jnp.int32(-1)
        for r in range(cap):
            current = jnp.int32(NONE)
            for block in blocks:
                current = jnp.minimum(current, jnp.where(block > previous, block, NONE))
            places = [p + jnp.where(current < b, 1, 0) for p, b in zip(places, blocks)]
            list_ref[row, r] = jnp.where(current < NONE, current, 0)
            previous = current
        for e in range(ENTRIES):
            place_ref[e] = jnp.minimum(places[e], cap - 1)

    for n in range(AHEAD_FWD):
        start_forward(n)
    work = [(u + q, part) for u in range(0, CHUNKS, 2) for q, part in ((0, 0), (1, 0), (0, 1), (0, 2), (1, 1), (1, 2))]
    for n in range(COUNT):
        if n + AHEAD_TWO < COUNT:
            start_two(n + AHEAD_TWO)
        if n + AHEAD_FWD < COUNT:
            start_forward(n + AHEAD_FWD)
        start_three(n)
        done = 0
        while work and done < 2:
            unit, part = work[0]
            if 4 * (unit // 2) + unit % 2 + (2 if part else 0) > n - LAG:
                break
            finish(*work.pop(0))
            done += 1 if part else 2
    while work:
        finish(*work.pop(0))
    for unit in range(CHUNKS):
        sibs[unit].wait_recv()
    for unit in (CHUNKS - 2, CHUNKS - 1):
        outs[unit].wait()
    for copy in sent:
        copy.wait_send()


def cross_spectra(cap, owner, tiles, traces):
    tail = (16, 128)
    dma = pltpu.SemaphoreType.DMA
    return pl.pallas_call(
        functools.partial(cross_kernel, cap),
        name=f"cross_{cap}",
        out_shape=jax.ShapeDtypeStruct((2 * CHUNKS, 4, BLOCK, 16, 128), BF16),
        in_specs=[
            pl.BlockSpec(memory_space=pltpu.SMEM),
            pl.BlockSpec(memory_space=pltpu.SMEM),
            pl.BlockSpec(memory_space=pl.ANY),
            pl.BlockSpec(memory_space=pl.ANY),
        ],
        out_specs=pl.BlockSpec(memory_space=pl.ANY),
        scratch_shapes=[pltpu.VMEM((4, 4, 8) + tail, BF16)] * COUNT
        + [pltpu.VMEM((4, cap, 4) + tail, BF16)] * COUNT
        + [pltpu.VMEM((3, cap, 4) + tail, BF16)] * STAGES
        + [pltpu.VMEM((2, 2, 4, BLOCK, 16, 128), BF16)]
        + [pltpu.VMEM((2, ENTRIES // 2, BLOCK, 8, 128), F32)]
        + [pltpu.SMEM((7, cap), jnp.int32), pltpu.SMEM((ENTRIES,), jnp.int32)]
        + [pltpu.VMEM((2, SAMPLES, 4 * BLOCK), BF16)]
        + [pltpu.VMEM((2 * BINS, SAMPLES), BF16)]
        + [pltpu.VMEM((4, GROUPS) + tail, BF16)]
        + [pltpu.VMEM((3, BINS, 128), F32)]
        + [dma((3,))]
        + [dma((COUNT,))] * 2
        + [dma((COUNT, 3))] * 2
        + [dma((COUNT, 2))] * 4
        + [dma((COUNT, 3))] * 2
        + [dma((CHUNKS,))] * 3,
        compiler_params=pltpu.CompilerParams(
            collective_id=cap, has_side_effects=True, vmem_limit_bytes=60 * 2**20
        ),
    )(owner, tiles, twiddles(), traces)


def turn_kernel(rows, owner_ref, cross_ref, out_ref):
    first = (lax.axis_index("src") * 16 + lax.axis_index("rcv")) * 4
    filled = owner_ref[first + pl.program_id(0)] < TILES

    @pl.when(filled)
    def _():
        @pl.loop(0, rows, unroll=16)
        def _(i):
            turned = cross_ref[:, 0, i].reshape(BINS, 128).T
            out_ref[0, i, :, :BINS] = turned[:BLOCK]
            out_ref[0, i, :, BINS:] = turned[BLOCK:]

    @pl.when(jnp.logical_not(filled))
    def _():
        out_ref[...] = jnp.zeros_like(out_ref)


def turn(owner, cross):
    rows = BLOCK
    return pl.pallas_call(
        functools.partial(turn_kernel, rows),
        name="turn",
        out_shape=jax.ShapeDtypeStruct((4, BLOCK, BLOCK, 2 * BINS), BF16),
        grid_spec=pltpu.PrefetchScalarGridSpec(
            num_scalar_prefetch=1,
            grid=(4, BLOCK // rows),
            in_specs=[pl.BlockSpec((2 * CHUNKS, 1, rows, 16, 128), lambda s, i, own: (0, s, i, 0, 0))],
            out_specs=pl.BlockSpec((1, rows, BLOCK, 2 * BINS), lambda s, i, own: (s, i, 0, 0)),
        ),
        compiler_params=pltpu.CompilerParams(vmem_limit_bytes=60 * 2**20),
    )(owner, cross)


def most_blocks(owner, tiles):
    ones = jnp.left_shift(1, tiles[:, 0]) | jnp.left_shift(1, tiles[:, 1])
    picked = owner[:, None] == jnp.arange(TILES, dtype=jnp.int32)[None, :]
    named = jnp.sum(jnp.where(picked, ones[None, :], 0), axis=1).reshape(4, 2, 16, 4)
    named = lax.reduce(named, np.int32(0), lax.bitwise_or, (1, 3))
    return jnp.max(lax.population_count(named))


def per_device(traces, tile_list, tile_owner):
    def run(cap):
        return lambda traces, tiles, owner: turn(owner, cross_spectra(cap, owner, tiles, traces))

    most = most_blocks(tile_owner, tile_list)
    index = sum((most > cap).astype(jnp.int32) for cap in CAPS[:-1])
    return lax.switch(index, [run(cap) for cap in CAPS], traces, tile_list.T, tile_owner)


def solution(mesh):
    in_specs = (P("rcv", "src"), P(), P())
    out_specs = P(("src", "rcv"), None, None, None)
    return jax.shard_map(
        per_device, mesh=mesh, in_specs=in_specs, out_specs=out_specs, check_vma=False
    )
```
